32 devices in a mesh: cluster: 4 (over z), sub: 8 (over y, x, core).
Axes of the slice: x: 2, y: 2, z: 4, core: 2. Of those that a mesh axis runs over, the one named last changes fastest.
Arguments:
- dual_operators: bfloat16 [64, 2048, 2048], P(('cluster', 'sub')), may hold values from -1 to 3, as said below
- local_loads: float32 [64, 2048, 128], P(('cluster', 'sub')), may hold values from -15 to 15
- modes: float32 [64, 6, 2048], P(('cluster', 'sub')), may hold values from -4 to 4
- coarse_matrix: float32 [384, 384], P(('cluster', 'sub')), may hold values from -1 to 1, as said below
- coarse_loads: float32 [384, 128], replicated, may hold values from -6144 to 6144
- slot_block: int32 [32, 32], P(('cluster', 'sub')), may hold values from 0 to 31, each once within a row
Outputs:
- multipliers: float32 [64, 2048, 128], P(('cluster', 'sub'))
- projected_residual: float32 [64, 2048, 128], P(('cluster', 'sub'))
The draws below stay inside these ranges and needn't reach their ends.
Inputs may be any that keep to these rules, and one draw needn't show every extreme that they name: `dual_operators`: each subdomain's matrix is symmetric and positive definite. `coarse_matrix`: Symmetric.
All inputs are finite; a program needn't handle non-finite values.
Results may differ from the reference program's by a relative error of at most 0.0018.
Values sent between devices are 32-bit elements; how exact they have to be, the bound alone decides.
A program may use at most 128 MiB of HBM per device.

```python
import math
import jax
import jax.numpy as jnp
from jax import lax

M = 2048
BLK = 128
NMODE = 6
LOADS = 128
ITERS = 3
NBD = 32
N_SUBDOM = 64
NC = 384
N_CLUSTER = 4
N_SUB = 8
DEVICES = 32


def symmetric_noise(noise_key, order):
    noise = jnp.clip(jax.random.normal(noise_key, (order, order), jnp.float32), -5.0, 5.0)
    return (noise + noise.T) / math.sqrt(2.0)


def draw_dual_operators(key, part):

    def one_matrix(index):
        noise_key, diag_key = jax.random.split(jax.random.fold_in(key, index))
        symmetric = symmetric_noise(noise_key, M) * (0.45 / math.sqrt(M))
        diagonal = jax.random.uniform(diag_key, (M,), jnp.float32, 1.0, 3.0)
        row_ids = lax.broadcasted_iota(jnp.int32, (M, M), 0)
        col_ids = lax.broadcasted_iota(jnp.int32, (M, M), 1)
        return jnp.where(row_ids == col_ids, diagonal[:, None], symmetric).astype(jnp.bfloat16)
    return lax.map(one_matrix, jnp.arange(N_SUBDOM, dtype=jnp.int32))


def draw_coarse_matrix(key, part):
    noise_key, diag_key = jax.random.split(jax.random.fold_in(key, 7))
    symmetric = symmetric_noise(noise_key, NC) * (0.5 / math.sqrt(NC) / M)
    diagonal = jnp.exp(jax.random.uniform(diag_key, (NC,), jnp.float32, math.log(0.5), math.log(2.0))) / M
    row_ids = lax.broadcasted_iota(jnp.int32, (NC, NC), 0)
    col_ids = lax.broadcasted_iota(jnp.int32, (NC, NC), 1)
    return jnp.where(row_ids == col_ids, diagonal[:, None], symmetric).astype(jnp.float32)


def draw_local_loads(key, part):
    noise_key = jax.random.fold_in(key, 11)
    noise = jnp.clip(jax.random.normal(noise_key, (N_SUBDOM, M, LOADS), jnp.float32), -5.0, 5.0)
    rising = 1.0 + 2.0 * jnp.arange(N_SUBDOM, dtype=jnp.float32) / (N_SUBDOM - 1)
    return (noise * rising[:, None, None]).astype(jnp.float32)


def level_of(stream_key, shape, pieces, low, largest):
    factor_of, own = 1.0, jax.random.fold_in(stream_key, 6)
    for axis_at, shards_of in pieces:
        draws = jnp.exp(jax.random.uniform(jax.random.fold_in(own, axis_at), (shards_of,), jnp.float32, low / len(pieces), largest / len(pieces)))
        factor_of = factor_of * jnp.repeat(draws, shape[axis_at] // shards_of).reshape([-1 if axis == axis_at else 1 for axis in range(len(shape))])
    return factor_of


def bell_draw(own_key, shape, spread, bound, pieces=(), kind=jnp.bfloat16):
    result = jax.random.normal(own_key, shape, jnp.float32) * spread
    if len(pieces) > 0:
        result = level_of(own_key, shape, pieces, -0.22, 0.18) * result
    return jnp.clip(result, min=-bound, max=bound).astype(kind)


def setup_inputs(seed: int = 0) -> dict:
    streams_of = jax.random.split(jax.random.key(seed), 7)
    dual_operators = draw_dual_operators(jax.random.fold_in(streams_of[6], 71), 0)
    local_loads = draw_local_loads(jax.random.fold_in(streams_of[6], 71), 0)
    modes = bell_draw(streams_of[2], (N_SUBDOM, NMODE, M), 1.0, 4.0, ((0, 32),), jnp.float32)
    coarse_matrix = draw_coarse_matrix(jax.random.fold_in(streams_of[6], 71), 0)
    coarse_loads = bell_draw(streams_of[4], (NC, LOADS), (0.5 * M), 6144.0, (), jnp.float32)
    slot_block = jax.vmap(lambda own: jax.random.permutation(own, NBD))(jax.random.split(streams_of[5], DEVICES)).reshape((DEVICES, NBD)).astype(jnp.int32)
    return {"dual_operators": dual_operators, "local_loads": local_loads, "modes": modes, "coarse_matrix": coarse_matrix, "coarse_loads": coarse_loads, "slot_block": slot_block}


def reference(dual_operators, local_loads, modes, coarse_matrix, coarse_loads, slot_block):
    highest = lax.Precision.HIGHEST
    device_total = N_CLUSTER * N_SUB
    block_total = slot_block.shape[1]
    face_size = block_total // 8
    positions = jnp.arange(block_total, dtype=jnp.int32)
    inverse = jnp.sum(positions[None, :, None] * (slot_block[:, :, None] == positions[None, None, :]).astype(jnp.int32), axis=1).astype(jnp.int32)
    device_ids = jnp.arange(device_total, dtype=jnp.int32)
    cluster_ids = (device_ids // N_SUB)[:, None]
    sub_ids = (device_ids % N_SUB)[:, None]
    face_ids = (positions // face_size)[None, :]
    shared = ((face_ids == 0) & (sub_ids > 0)) | ((face_ids == 1) & (sub_ids < N_SUB - 1)) | ((face_ids == 2) & (cluster_ids > 0)) | ((face_ids == 3) & (cluster_ids < N_CLUSTER - 1)) | (face_ids >= 6)
    slot_weights = jnp.where(shared, 0.5, 1.0).astype(jnp.float32)
    weights = jnp.repeat(jnp.take_along_axis(slot_weights, inverse, axis=1), BLK, axis=1).reshape(N_SUBDOM, M)

    def receive(slot_grid):
        def face_slots(index):
            return slot_grid[:, :, index * face_size:(index + 1) * face_size]

        blank_faces = jnp.zeros_like(face_slots(0))
        lower_sub = jnp.concatenate([blank_faces[:, :1], face_slots(1)[:, :-1]], axis=1)
        upper_sub = jnp.concatenate([face_slots(0)[:, 1:], blank_faces[:, :1]], axis=1)
        lower_cluster = jnp.concatenate([blank_faces[:1], face_slots(3)[:-1]], axis=0)
        upper_cluster = jnp.concatenate([face_slots(2)[1:], blank_faces[:1]], axis=0)
        return jnp.concatenate([lower_sub, upper_sub, lower_cluster, upper_cluster, blank_faces, blank_faces, face_slots(7), face_slots(6)], axis=2)

    def assemble(values):
        width_now = values.shape[-1]
        blocks = values.reshape(device_total, block_total, BLK, width_now)
        sent = jnp.take_along_axis(blocks, slot_block[:, :, None, None], axis=1)
        slot_grid = sent.reshape(N_CLUSTER, N_SUB, block_total, BLK, width_now)
        received = receive(slot_grid).reshape(sent.shape)
        assembled = jnp.take_along_axis(sent - received, inverse[:, :, None, None], axis=1)
        return assembled.reshape(N_SUBDOM, M, width_now)

    def apply_dual(direction):
        rounded = lax.optimization_barrier(direction.astype(jnp.bfloat16)).astype(jnp.float32)

        def apply_one(paired):
            return jnp.dot(paired[0].astype(jnp.float32), paired[1], precision=highest)

        return assemble(lax.map(apply_one, (dual_operators, rounded)))

    def coarse_coefficients(values):
        coarse_terms = jnp.einsum("srm,sml->srl", modes, values, precision=highest).reshape(NC, LOADS)
        return jnp.dot(coarse_matrix, coarse_terms, precision=highest)

    def spread_modes(coeff):
        return jnp.einsum("srm,srl->sml", modes, coeff.reshape(N_SUBDOM, NMODE, LOADS), precision=highest)

    def project(values):
        return values - assemble(spread_modes(coarse_coefficients(values)))

    def inner_product(left, right):
        return jnp.sum(weights[:, :, None] * left * right, axis=(0, 1))

    dual_rhs = assemble(local_loads)
    multipliers = assemble(spread_modes(jnp.dot(coarse_matrix, coarse_loads, precision=highest)))
    residual = dual_rhs - apply_dual(multipliers)
    projected = project(residual)
    gamma_now = inner_product(projected, projected)
    direction = projected
    for iteration in range(ITERS):
        image_dir = apply_dual(direction)
        step_size = gamma_now / inner_product(direction, image_dir)
        multipliers = multipliers + step_size * direction
        residual = residual - step_size * image_dir
        projected = project(residual)
        if iteration + 1 < ITERS:
            gamma_next = inner_product(projected, projected)
            direction = projected + (gamma_next / gamma_now) * direction
            gamma_now = gamma_next
    return (multipliers, projected)
```

```python
import functools

import jax
import jax.numpy as jnp
from jax import lax
from jax.experimental import pallas as pl
from jax.experimental.pallas import tpu as pltpu
from jax.sharding import PartitionSpec as P

ITERS = 3
PAD = 8
LANES = 128
MESH = pl.DeviceIdType.MESH
F32, BF16 = jnp.float32, jnp.bfloat16


def split(x):
    high = x.astype(BF16)
    return high, (x - high.astype(F32)).astype(BF16)


def rows8(x):
    return jnp.sum(x.reshape(-1, 8, x.shape[-1]), axis=0)


def kernel(
    nc, ns, parts, face,
    slot_ref, inv_ref, ops_hbm, loads_hbm, modes_ref, cmat_ref, cload_ref,
    mult_out, proj_out,
    ops, ybuf, img, res, proj, dire, mult, emat, vb, halo, mslot, mfetch, mhl, call, hall, gz, gs,
    ops_sem, loads_sem, halo_send, halo_recv, m_send, m_recv, c_send, c_recv,
    zsend, zrecv, ssend, srecv, gzrecv, gsrecv,
):
    c, i = lax.axis_index("cluster"), lax.axis_index("sub")
    nblk = 8 * face
    per = nblk // parts
    blk = ybuf.shape[1]
    frows = face * blk
    unit = parts * PAD

    ops_copy = pltpu.make_async_copy(ops_hbm, ops, ops_sem)
    ops_copy.start()
    loads_copy = pltpu.make_async_copy(loads_hbm, proj, loads_sem)
    loads_copy.start()

    barrier = pltpu.get_barrier_semaphore()
    for k in range(1, nc):
        pl.semaphore_signal(barrier, inc=1, device_id=(lax.rem(c + k, nc), i), device_id_type=MESH)
    for k in range(1, ns):
        pl.semaphore_signal(barrier, inc=1, device_id=(c, lax.rem(i + k, ns)), device_id_type=MESH)

    for j in range(nblk):
        b = slot_ref[j]
        piece = modes_ref[b]
        block = jnp.broadcast_to(b, piece.shape)
        for own in range(parts):
            mine = (block >= own * per) & (block < (own + 1) * per)
            mslot[j, own * PAD:(own + 1) * PAD, :] = jnp.where(mine, piece, 0.0)
    call[0] = cmat_ref[...]

    def partner(f):
        axis, sign = f // 2, 2 * (f % 2) - 1
        tc, ti = c + axis * sign, i + (1 - axis) * sign
        there = (tc >= 0) & (tc < nc) & (ti >= 0) & (ti < ns)
        return there, (tc, ti), axis * 2 + 1 - f % 2

    def halo_copy(f, landing):
        _, device, _ = partner(f)
        return pltpu.make_async_remote_copy(
            src_ref=ybuf.at[pl.ds(f * face, face)], dst_ref=halo.at[landing],
            send_sem=halo_send.at[f], recv_sem=halo_recv.at[landing],
            device_id=device, device_id_type=MESH)

    def mode_copy(f, landing):
        _, device, _ = partner(f)
        return pltpu.make_async_remote_copy(
            src_ref=mslot.at[pl.ds(f * face, face)], dst_ref=mfetch.at[landing],
            send_sem=m_send.at[f], recv_sem=m_recv.at[landing],
            device_id=device, device_id_type=MESH)

    def coarse_copy(f, landing):
        _, device, _ = partner(f)
        return pltpu.make_async_remote_copy(
            src_ref=call.at[0], dst_ref=call.at[landing + 1],
            send_sem=c_send.at[f], recv_sem=c_recv.at[landing],
            device_id=device, device_id_type=MESH)

    pl.semaphore_wait(barrier, nc + ns - 2)
    for f in range(4):
        there, _, landing = partner(f)

        @pl.when(there)
        def _():
            mode_copy(f, landing).start()
            coarse_copy(f, landing).start()

        @pl.when(jnp.logical_not(there))
        def _():
            halo[f] = jnp.zeros(halo.shape[1:], F32)
            mfetch[f] = jnp.zeros(mfetch.shape[1:], F32)
            call[f + 1] = jnp.zeros(call.shape[1:], F32)

    for g in range(8):
        for k in range(face):
            high, low = split(mslot[g * face + k])
            mhl[g, 0:unit, k * blk:(k + 1) * blk] = high
            mhl[g, unit:2 * unit, k * blk:(k + 1) * blk] = low

    for f in range(4):
        there, _, _ = partner(f)

        @pl.when(there)
        def _():
            mode_copy(f, f).wait_recv()
            coarse_copy(f, f).wait_recv()
            mode_copy(f, f).wait_send()
            coarse_copy(f, f).wait_send()

    for g in range(8):
        for k in range(face):
            j = g * face + k
            own = mslot[j]
            if g == 6:
                own = own - mslot[j + face]
            if g == 7:
                own = own - mslot[j - face]
            pieces = [own]
            if g < 4:
                if g > 0:
                    pieces.append(jnp.zeros((g * unit, blk), F32))
                pieces.append(-mfetch[g, k])
            used = sum(x.shape[0] for x in pieces)
            pieces.append(jnp.zeros((LANES - used, blk), F32))
            high, low = split(jnp.concatenate(pieces, axis=0).T)
            emat[g, k * blk:(k + 1) * blk, 0:LANES] = high
            emat[g, k * blk:(k + 1) * blk, LANES:] = low

    cfull = call[...].reshape(5 * unit, call.shape[-1])

    def coarse(terms):
        return jnp.dot(cfull, terms, precision=lax.Precision.HIGHEST, preferred_element_type=F32)

    def spread_side(coeff):
        high, low = split(jnp.concatenate(
            [coeff, jnp.zeros((LANES - coeff.shape[0], coeff.shape[1]), F32)], axis=0))
        top = jnp.concatenate([high, low], axis=1)
        bottom = jnp.concatenate([high, jnp.zeros_like(low)], axis=1)
        return jnp.concatenate([top, bottom], axis=0)

    def correct(g, side):
        both = jnp.dot(emat[g], side, preferred_element_type=F32)
        width = both.shape[1] // 2
        return both[:, :width] + both[:, width:]

    def at(ref, g):
        return ref[pl.ds(g * face, face)].reshape(frows, ref.shape[-1])

    def put(ref, g, value):
        ref[pl.ds(g * face, face)] = value.reshape(face, blk, value.shape[-1])

    width = ybuf.shape[-1]

    def load_side(source):
        for b in range(nblk):
            t, r = b // per, b % per
            vb[r * blk:(r + 1) * blk, t * width:(t + 1) * width] = source[inv_ref[b]].astype(BF16)

    def product(g):
        pieces, blocks = [], []
        for k in range(face):
            b = slot_ref[g * face + k]
            pieces.append(ops[b])
            blocks.append(jnp.broadcast_to(b, (blk, width)))
        wide = jnp.dot(jnp.concatenate(pieces, axis=0), vb[...], preferred_element_type=F32)
        block = jnp.concatenate(blocks, axis=0)
        value = wide[:, :width]
        for t in range(1, parts):
            value = jnp.where(block >= t * per, wide[:, t * width:(t + 1) * width], value)
        return value

    def start_halo(f):
        there, _, landing = partner(f)

        @pl.when(there)
        def _():
            halo_copy(f, landing).start()

    def wait_halo():
        for f in (0, 1, 2, 3):
            there, _, _ = partner(f)

            @pl.when(there)
            def _():
                halo_copy(f, f).wait_recv()

    def wait_halo_sent():
        for f in range(4):
            there, _, _ = partner(f)

            @pl.when(there)
            def _():
                halo_copy(f, f).wait_send()

    def assembled(g):
        mine = at(ybuf, g)
        if g < 4:
            return mine - halo[g].reshape(frows, width)
        if g < 6:
            return mine
        return mine - at(ybuf, 13 - g)

    def terms_of(g, value):
        high, low = split(value)
        return jnp.dot(mhl[g], jnp.concatenate([high, low], axis=1), preferred_element_type=F32)

    def fold(both):
        return both[:unit, :width] + (both[:unit, width:] + both[unit:, :width])

    def weight(g):
        if g < 4:
            there, _, _ = partner(g)
            return jnp.where(there, 0.5, 1.0).astype(F32)
        return 1.0 if g < 6 else 0.5

    def gather(par, terms):
        hall[par, c, i] = terms
        zs, ss = [], []
        for k in range(1, nc):
            zs.append(pltpu.make_async_remote_copy(
                src_ref=hall.at[par, c, i], dst_ref=hall.at[par, c, i],
                send_sem=zsend.at[k], recv_sem=zrecv.at[par, c],
                device_id=(lax.rem(c + k, nc), i), device_id_type=MESH))
        for copy in zs:
            copy.start()
        for k in range(1, nc):
            peer = lax.rem(c + k, nc)
            pltpu.make_async_remote_copy(
                src_ref=hall.at[par, peer, i], dst_ref=hall.at[par, peer, i],
                send_sem=zsend.at[k], recv_sem=zrecv.at[par, peer],
                device_id=(peer, i), device_id_type=MESH).wait_recv()
        for k in range(1, ns):
            ss.append(pltpu.make_async_remote_copy(
                src_ref=hall.at[par, :, i], dst_ref=hall.at[par, :, i],
                send_sem=ssend.at[k], recv_sem=srecv.at[par, i],
                device_id=(c, lax.rem(i + k, ns)), device_id_type=MESH))
        for copy in ss:
            copy.start()
        for k in range(1, ns):
            peer = lax.rem(i + k, ns)
            pltpu.make_async_remote_copy(
                src_ref=hall.at[par, :, peer], dst_ref=hall.at[par, :, peer],
                send_sem=ssend.at[k], recv_sem=srecv.at[par, peer],
                device_id=(c, peer), device_id_type=MESH).wait_recv()
        for copy in zs + ss:
            copy.wait_send()
        whole = hall[par].reshape(nc * ns, unit, width)
        return jnp.sum(whole, axis=0), coarse(whole.reshape(nc * ns * unit, width))

    def total(value):
        gz[c] = value
        zs, ss = [], []
        for k in range(1, nc):
            zs.append(pltpu.make_async_remote_copy(
                src_ref=gz.at[c], dst_ref=gz.at[c], send_sem=zsend.at[k], recv_sem=gzrecv.at[c],
                device_id=(lax.rem(c + k, nc), i), device_id_type=MESH))
        for copy in zs:
            copy.start()
        for k in range(1, nc):
            peer = lax.rem(c + k, nc)
            pltpu.make_async_remote_copy(
                src_ref=gz.at[peer], dst_ref=gz.at[peer], send_sem=zsend.at[k], recv_sem=gzrecv.at[peer],
                device_id=(peer, i), device_id_type=MESH).wait_recv()
        gs[i] = jnp.sum(gz[...], axis=0)
        for k in range(1, ns):
            ss.append(pltpu.make_async_remote_copy(
                src_ref=gs.at[i], dst_ref=gs.at[i], send_sem=ssend.at[k], recv_sem=gsrecv.at[i],
                device_id=(c, lax.rem(i + k, ns)), device_id_type=MESH))
        for copy in ss:
            copy.start()
        for k in range(1, ns):
            peer = lax.rem(i + k, ns)
            pltpu.make_async_remote_copy(
                src_ref=gs.at[peer], dst_ref=gs.at[peer], send_sem=ssend.at[k], recv_sem=gsrecv.at[peer],
                device_id=(c, peer), device_id_type=MESH).wait_recv()
        for copy in zs + ss:
            copy.wait_send()
        return jnp.sum(jnp.sum(gs[...], axis=0), axis=0, keepdims=True)

    row_ids = lax.broadcasted_iota(jnp.int32, (unit, width), 0)

    side = spread_side(coarse(cload_ref[...]))
    for g in range(8):
        put(mult, g, correct(g, side))
    load_side(mult)
    loads_copy.wait()
    ops_copy.wait()

    def loads_at(g):
        return jnp.concatenate([proj[slot_ref[g * face + k]] for k in range(face)], axis=0)

    def first_outer(step, carry):
        f = (step + 2) % 4
        put(ybuf, f, loads_at(f) - product(f))
        start_halo(f)
        return carry

    def first_inner(g, carry):
        put(ybuf, g, loads_at(g) - product(g))
        return carry

    lax.fori_loop(0, 4, first_outer, 0)
    lax.fori_loop(4, 8, first_inner, 0)
    terms = jnp.zeros((2 * unit, 2 * width), F32)
    wait_halo()
    for g in (4, 5, 6, 7, 0, 1, 2, 3):
        value = assembled(g)
        put(res, g, value)
        terms = terms + terms_of(g, value)
    wait_halo_sent()
    _, coeff = gather(0, fold(terms))
    side = spread_side(coeff)
    part = jnp.zeros((8, width), F32)
    for g in range(8):
        value = at(res, g) - correct(g, side)
        put(dire, g, value)
        part = part + weight(g) * rows8(value * value)
    gamma = None

    for iteration in range(ITERS):
        load_side(dire)

        def outer(step, carry):
            f = (step + 2) % 4
            value = product(f)
            put(ybuf, f, value)
            start_halo(f)
            return carry + rows8(value * at(dire, f))

        def inner(g, carry):
            value = product(g)
            put(ybuf, g, value)
            return carry + rows8(value * at(dire, g))

        curv = lax.fori_loop(0, 4, outer, jnp.zeros((8, width), F32))
        curv = lax.fori_loop(4, 8, inner, curv)
        curv = jnp.sum(curv, axis=0, keepdims=True)
        terms = jnp.zeros((2 * unit, 2 * width), F32)
        wait_halo()
        for g in (4, 5, 6, 7, 0, 1, 2, 3):
            value = assembled(g)
            put(img, g, value)
            terms = terms + terms_of(g, value)
        wait_halo_sent()
        message = jnp.where(row_ids == PAD - 2, curv, fold(terms))
        if gamma is None:
            message = jnp.where(row_ids == PAD - 1, jnp.sum(part, axis=0, keepdims=True), message)
        sums, coeff_image = gather((iteration + 1) % 2, message)
        if gamma is None:
            gamma = sums[PAD - 1:PAD]
        length = gamma / sums[PAD - 2:PAD - 1]
        coeff = coeff - length * coeff_image
        side = spread_side(coeff)
        last = iteration + 1 == ITERS
        part = jnp.zeros((8, width), F32)
        for g in range(8):
            put(mult, g, at(mult, g) + length * at(dire, g))
            value = at(res, g) - length * at(img, g)
            if not last:
                put(res, g, value)
            value = value - correct(g, side)
            put(proj, g, value)
            if not last:
                part = part + weight(g) * rows8(value * value)
        if not last:
            following = total(part)
            ratio = following / gamma
            gamma = following
            for g in range(8):
                put(dire, g, at(proj, g) + ratio * at(dire, g))

    for b in range(nblk):
        mult_out[b] = mult[inv_ref[b]]
        proj_out[b] = proj[inv_ref[b]]


def solution(mesh):
    nc, ns = mesh.shape["cluster"], mesh.shape["sub"]
    devices = nc * ns

    def on_device(dual_operators, local_loads, modes, coarse_matrix, coarse_loads, slot_block):
        parts, order, loads = local_loads.shape
        nmode = modes.shape[1]
        slots = slot_block[0]
        nblk = slots.shape[0]
        face = nblk // 8
        blk = order * parts // nblk
        unit = parts * PAD
        positions = jnp.arange(nblk, dtype=jnp.int32)
        inverse = jnp.sum(
            positions[:, None] * (slots[:, None] == positions[None, :]).astype(jnp.int32), axis=0)
        extra = PAD - nmode
        per = nblk // parts
        modes8 = jnp.pad(
            modes.reshape(parts, nmode, per, blk).transpose(0, 2, 1, 3).reshape(nblk, nmode, blk),
            ((0, 0), (0, extra), (0, 0)))
        cmat = jnp.pad(
            coarse_matrix.reshape(parts, nmode, devices * parts, nmode),
            ((0, 0), (0, extra), (0, 0), (0, extra))).reshape(unit, devices * unit)
        cload = jnp.pad(
            coarse_loads.reshape(devices * parts, nmode, loads),
            ((0, 0), (0, extra), (0, 0))).reshape(devices * unit, loads)
        vmem = pl.BlockSpec(memory_space=pltpu.VMEM)
        smem = pl.BlockSpec(memory_space=pltpu.SMEM)
        anym = pl.BlockSpec(memory_space=pl.ANY)
        vec = pltpu.VMEM((nblk, blk, loads), F32)
        dma = pltpu.SemaphoreType.DMA
        out = jax.ShapeDtypeStruct((nblk, blk, loads), F32)
        mult, proj = pl.pallas_call(
            functools.partial(kernel, nc, ns, parts, face),
            out_shape=(out, out),
            in_specs=[smem, smem, anym, anym, vmem, vmem, vmem],
            out_specs=(vmem, vmem),
            scratch_shapes=[
                pltpu.VMEM((nblk, blk, order), BF16),
                vec, vec, vec, vec, vec, vec,
                pltpu.VMEM((8, face * blk, 2 * LANES), BF16),
                pltpu.VMEM((order, parts * loads), BF16),
                pltpu.VMEM((4, face, blk, loads), F32),
                pltpu.VMEM((nblk, unit, blk), F32),
                pltpu.VMEM((4, face, unit, blk), F32),
                pltpu.VMEM((8, 2 * unit, face * blk), BF16),
                pltpu.VMEM((5, unit, devices * unit), F32),
                pltpu.VMEM((2, nc, ns, unit, loads), F32),
                pltpu.VMEM((nc, 8, loads), F32),
                pltpu.VMEM((ns, 8, loads), F32),
                dma(()), dma(()),
                dma((4,)), dma((4,)), dma((4,)), dma((4,)), dma((4,)), dma((4,)),
                dma((nc,)), dma((2, nc)), dma((ns,)), dma((2, ns)), dma((nc,)), dma((ns,)),
            ],
            compiler_params=pltpu.CompilerParams(
                collective_id=0, has_side_effects=True, vmem_limit_bytes=56 * 1024 * 1024),
            cost_estimate=pl.CostEstimate(
                flops=8 * parts * order * order * loads, bytes_accessed=24 * 1024 * 1024, transcendentals=0),
        )(slots, inverse, dual_operators.reshape(nblk, blk, order), local_loads.reshape(nblk, blk, loads), modes8, cmat, cload)
        return mult.reshape(local_loads.shape), proj.reshape(local_loads.shape)

    return jax.shard_map(
        on_device,
        mesh=mesh,
        in_specs=(
            P(("cluster", "sub"), None, None),
            P(("cluster", "sub"), None, None),
            P(("cluster", "sub"), None, None),
            P(("cluster", "sub"), None),
            P(),
            P(("cluster", "sub"), None),
        ),
        out_specs=(P(("cluster", "sub"), None, None), P(("cluster", "sub"), None, None)),
        check_vma=False,
    )
```

```python
import functools

import jax
import jax.numpy as jnp
from jax import lax
from jax.experimental import pallas as pl
from jax.experimental.pallas import tpu as pltpu
from jax.sharding import PartitionSpec as P

ITERS = 3
PAD = 8
LANES = 128
MESH = pl.DeviceIdType.MESH
F32, BF16 = jnp.float32, jnp.bfloat16


def split(x):
    high = x.astype(BF16)
    return high, (x - high.astype(F32)).astype(BF16)


def rows8(x):
    return jnp.sum(x.reshape(-1, 8, x.shape[-1]), axis=0)


def kernel(
    nc, ns, parts, face,
    slot_ref, inv_ref, ops_hbm, loads_hbm, modes_ref, cmat_ref, cload_ref,
    mult_out, proj_out,
    ops, ybuf, res, proj, dire, mult, emat, vb, halo, mraw, mslot, mfetch, mhl, call, cpad, hall, gz, gs,
    ops_sem, loads_sem, halo_send, halo_recv, m_send, m_recv, c_send, c_recv,
    zsend, zrecv, ssend, srecv, gzrecv, gsrecv,
):
    c, i = lax.axis_index("cluster"), lax.axis_index("sub")
    nblk = 8 * face
    per = nblk // parts
    blk = ybuf.shape[1]
    frows = face * blk
    unit = parts * PAD
    width = ybuf.shape[-1]

    nmode = modes_ref.shape[1]
    ops_copies = [
        pltpu.make_async_copy(
            ops_hbm.at[pl.ds(k * face, face)], ops.at[pl.ds(k * face, face)], ops_sem.at[k])
        for k in range(8)]
    for copy in ops_copies:
        copy.start()
    loads_copy = pltpu.make_async_copy(loads_hbm, proj, loads_sem)
    loads_copy.start()

    barrier = pltpu.get_barrier_semaphore()
    for k in range(1, nc):
        pl.semaphore_signal(barrier, inc=1, device_id=(lax.rem(c + k, nc), i), device_id_type=MESH)
    for k in range(1, ns):
        pl.semaphore_signal(barrier, inc=1, device_id=(c, lax.rem(i + k, ns)), device_id_type=MESH)

    mraw[...] = jnp.zeros_like(mraw)
    for b in range(nblk):
        t, r = b // per, b % per
        mraw[b, 0:nmode, :] = modes_ref[t, :, r * blk:(r + 1) * blk]
    for j in range(nblk):
        b = slot_ref[0, j]
        piece = mraw[b]
        block = jnp.broadcast_to(b, piece.shape)
        for own in range(parts):
            mine = (block >= own * per) & (block < (own + 1) * per)
            mslot[j, own * PAD:(own + 1) * PAD, :] = jnp.where(mine, piece, 0.0)
    call[0] = jnp.zeros(call.shape[1:], F32)
    for t in range(parts):
        call[0, t * PAD:t * PAD + nmode, :] = cmat_ref[t * nmode:(t + 1) * nmode, :]

    def partner(f):
        axis, sign = f // 2, 2 * (f % 2) - 1
        tc, ti = c + axis * sign, i + (1 - axis) * sign
        there = (tc >= 0) & (tc < nc) & (ti >= 0) & (ti < ns)
        return there, (tc, ti), axis * 2 + 1 - f % 2

    def halo_copy(f, landing, par):
        _, device, _ = partner(f)
        return pltpu.make_async_remote_copy(
            src_ref=ybuf.at[pl.ds(f * face, face)], dst_ref=halo.at[par, landing],
            send_sem=halo_send.at[f], recv_sem=halo_recv.at[par, landing],
            device_id=device, device_id_type=MESH)

    def mode_copy(f, landing):
        _, device, _ = partner(f)
        return pltpu.make_async_remote_copy(
            src_ref=mslot.at[pl.ds(f * face, face)], dst_ref=mfetch.at[landing],
            send_sem=m_send.at[f], recv_sem=m_recv.at[landing],
            device_id=device, device_id_type=MESH)

    def coarse_copy(f, landing):
        _, device, _ = partner(f)
        return pltpu.make_async_remote_copy(
            src_ref=call.at[0], dst_ref=call.at[landing + 1],
            send_sem=c_send.at[f], recv_sem=c_recv.at[landing],
            device_id=device, device_id_type=MESH)

    pl.semaphore_wait(barrier, nc + ns - 2)
    for f in range(4):
        there, _, landing = partner(f)

        @pl.when(there)
        def _():
            mode_copy(f, landing).start()
            coarse_copy(f, landing).start()

        @pl.when(jnp.logical_not(there))
        def _():
            halo[0, f] = jnp.zeros(halo.shape[2:], F32)
            halo[1, f] = jnp.zeros(halo.shape[2:], F32)
            mfetch[f] = jnp.zeros(mfetch.shape[1:], F32)
            call[f + 1] = jnp.zeros(call.shape[1:], F32)

    for g in range(8):
        for k in range(face):
            j = g * face + k
            own = mslot[j]
            if g == 6:
                own = own - mslot[j + face]
            if g == 7:
                own = own - mslot[j - face]
            high, low = split(own)
            mhl[g, 0:unit, k * blk:(k + 1) * blk] = high
            mhl[g, unit:2 * unit, k * blk:(k + 1) * blk] = low

    for f in range(4):
        there, _, _ = partner(f)

        @pl.when(there)
        def _():
            mode_copy(f, f).wait_recv()
            coarse_copy(f, f).wait_recv()
            mode_copy(f, f).wait_send()
            coarse_copy(f, f).wait_send()

    for g in range(8):
        for k in range(face):
            j = g * face + k
            own = mslot[j]
            if g == 6:
                own = own - mslot[j + face]
            if g == 7:
                own = own - mslot[j - face]
            pieces = [own]
            if g < 4:
                if g > 0:
                    pieces.append(jnp.zeros((g * unit, blk), F32))
                pieces.append(-mfetch[g, k])
            used = sum(x.shape[0] for x in pieces)
            pieces.append(jnp.zeros((LANES - used, blk), F32))
            high, low = split(jnp.concatenate(pieces, axis=0).T)
            emat[g, k * blk:(k + 1) * blk, 0:LANES] = high
            emat[g, k * blk:(k + 1) * blk, LANES:] = low

    highest = lax.Precision.HIGHEST
    cfull = call[...].reshape(5 * unit, call.shape[-1])
    first = jnp.dot(cfull, cload_ref[...], precision=highest, preferred_element_type=F32)
    columns = call.shape[-1]
    chunk = nmode * LANES // 2
    if columns % chunk:
        chunk = columns
    padded = chunk // nmode * PAD
    place_rows = lax.broadcasted_iota(jnp.int32, (chunk, padded), 0)
    place_cols = lax.broadcasted_iota(jnp.int32, (chunk, padded), 1)
    group, mode = place_cols >> 3, place_cols & (PAD - 1)
    place = jnp.where((place_rows == group * nmode + mode) & (mode < nmode), 1.0, 0.0).astype(F32)
    for k in range(columns // chunk):
        high, low = split(jnp.dot(
            cfull[:, k * chunk:(k + 1) * chunk], place, precision=highest, preferred_element_type=F32))
        cpad[0:5 * unit, k * padded:(k + 1) * padded] = high
        cpad[5 * unit:10 * unit, k * padded:(k + 1) * padded] = low

    def coarse(terms):
        high, low = split(terms)
        both = jnp.dot(cpad[...], jnp.concatenate([high, low], axis=1), preferred_element_type=F32)
        top = 5 * unit
        return both[:top, :width] + (both[:top, width:] + both[top:, :width])

    def spread_side(coeff):
        high, low = split(jnp.concatenate(
            [coeff, jnp.zeros((LANES - coeff.shape[0], coeff.shape[1]), F32)], axis=0))
        top = jnp.concatenate([high, low], axis=1)
        bottom = jnp.concatenate([high, jnp.zeros_like(low)], axis=1)
        return jnp.concatenate([top, bottom], axis=0)

    def correct(g, side):
        both = jnp.dot(emat[g], side, preferred_element_type=F32)
        width = both.shape[1] // 2
        return both[:, :width] + both[:, width:]

    def at(ref, g):
        return ref[pl.ds(g * face, face)].reshape(frows, ref.shape[-1])

    def put(ref, g, value):
        ref[pl.ds(g * face, face)] = value.reshape(face, blk, value.shape[-1])

    def load_side(source):
        for b in range(nblk):
            t, r = b // per, b % per
            vb[r * blk:(r + 1) * blk, t * width:(t + 1) * width] = source[inv_ref[b]].astype(BF16)

    def product(g):
        pieces, blocks = [], []
        for k in range(face):
            b = slot_ref[0, g * face + k]
            pieces.append(ops[b])
            blocks.append(jnp.broadcast_to(b, (blk, width)))
        wide = jnp.dot(jnp.concatenate(pieces, axis=0), vb[...], preferred_element_type=F32)
        block = jnp.concatenate(blocks, axis=0)
        value = wide[:, :width]
        for t in range(1, parts):
            value = jnp.where(block >= t * per, wide[:, t * width:(t + 1) * width], value)
        return value

    def start_halo(f, par):
        there, _, landing = partner(f)

        @pl.when(there)
        def _():
            halo_copy(f, landing, par).start()

    def wait_halo(f, par):
        there, _, _ = partner(f)

        @pl.when(there)
        def _():
            halo_copy(f, f, par).wait_recv()

    def wait_halo_sent(par):
        for f in range(4):
            there, _, _ = partner(f)

            @pl.when(there)
            def _():
                halo_copy(f, f, par).wait_send()

    def assembled(g, par):
        mine = at(ybuf, g)
        if g < 4:
            return mine - halo[par, g].reshape(frows, width)
        if g < 6:
            return mine
        return mine - at(ybuf, 13 - g)

    def terms_of(g, value):
        high, low = split(value)
        return jnp.dot(mhl[g], jnp.concatenate([high, low], axis=1), preferred_element_type=F32)

    def image_terms(par):
        terms = lax.fori_loop(
            0, 8, lambda g, carry: carry + terms_of(g, at(ybuf, g)),
            jnp.zeros((2 * unit, 2 * width), F32))
        for f in range(4):
            wait_halo(f, par)
            terms = terms - terms_of(f, halo[par, f].reshape(frows, width))
        return terms

    def fold(both):
        return both[:unit, :width] + (both[:unit, width:] + both[unit:, :width])

    def weight(g):
        if g < 4:
            there, _, _ = partner(g)
            return jnp.where(there, 0.5, 1.0).astype(F32)
        return 1.0 if g < 6 else 0.5

    def gather(par, terms):
        hall[par, c, i] = terms
        zs, ss = [], []
        for k in range(1, nc):
            zs.append(pltpu.make_async_remote_copy(
                src_ref=hall.at[par, c, i], dst_ref=hall.at[par, c, i],
                send_sem=zsend.at[k], recv_sem=zrecv.at[par, c],
                device_id=(lax.rem(c + k, nc), i), device_id_type=MESH))
        for copy in zs:
            copy.start()
        for k in range(1, nc):
            peer = lax.rem(c + k, nc)
            pltpu.make_async_remote_copy(
                src_ref=hall.at[par, peer, i], dst_ref=hall.at[par, peer, i],
                send_sem=zsend.at[k], recv_sem=zrecv.at[par, peer],
                device_id=(peer, i), device_id_type=MESH).wait_recv()
        for k in range(1, ns):
            ss.append(pltpu.make_async_remote_copy(
                src_ref=hall.at[par, :, i], dst_ref=hall.at[par, :, i],
                send_sem=ssend.at[k], recv_sem=srecv.at[par, i],
                device_id=(c, lax.rem(i + k, ns)), device_id_type=MESH))
        for copy in ss:
            copy.start()
        for k in range(1, ns):
            peer = lax.rem(i + k, ns)
            pltpu.make_async_remote_copy(
                src_ref=hall.at[par, :, peer], dst_ref=hall.at[par, :, peer],
                send_sem=ssend.at[k], recv_sem=srecv.at[par, peer],
                device_id=(c, peer), device_id_type=MESH).wait_recv()
        for copy in zs + ss:
            copy.wait_send()
        whole = hall[par].reshape(nc * ns, unit, width)
        return jnp.sum(whole, axis=0), coarse(whole.reshape(nc * ns * unit, width))

    def total(value, meanwhile):
        gz[c] = value
        zs, ss = [], []
        for k in range(1, nc):
            zs.append(pltpu.make_async_remote_copy(
                src_ref=gz.at[c], dst_ref=gz.at[c], send_sem=zsend.at[k], recv_sem=gzrecv.at[c],
                device_id=(lax.rem(c + k, nc), i), device_id_type=MESH))
        for copy in zs:
            copy.start()
        meanwhile()
        for k in range(1, nc):
            peer = lax.rem(c + k, nc)
            pltpu.make_async_remote_copy(
                src_ref=gz.at[peer], dst_ref=gz.at[peer], send_sem=zsend.at[k], recv_sem=gzrecv.at[peer],
                device_id=(peer, i), device_id_type=MESH).wait_recv()
        gs[i] = jnp.sum(gz[...], axis=0)
        for k in range(1, ns):
            ss.append(pltpu.make_async_remote_copy(
                src_ref=gs.at[i], dst_ref=gs.at[i], send_sem=ssend.at[k], recv_sem=gsrecv.at[i],
                device_id=(c, lax.rem(i + k, ns)), device_id_type=MESH))
        for copy in ss:
            copy.start()
        for k in range(1, ns):
            peer = lax.rem(i + k, ns)
            pltpu.make_async_remote_copy(
                src_ref=gs.at[peer], dst_ref=gs.at[peer], send_sem=ssend.at[k], recv_sem=gsrecv.at[peer],
                device_id=(c, peer), device_id_type=MESH).wait_recv()
        for copy in zs + ss:
            copy.wait_send()
        return jnp.sum(jnp.sum(gs[...], axis=0), axis=0, keepdims=True)

    row_ids = lax.broadcasted_iota(jnp.int32, (unit, width), 0)

    side = spread_side(first)
    for g in range(8):
        put(mult, g, correct(g, side))
    load_side(mult)
    loads_copy.wait()
    for copy in ops_copies:
        copy.wait()

    def loads_at(g):
        return jnp.concatenate([proj[slot_ref[0, g * face + k]] for k in range(face)], axis=0)

    def first_outer(step, carry):
        f = (step + 2) % 4
        put(ybuf, f, loads_at(f) - product(f))
        start_halo(f, 0)
        return carry

    def first_inner(g, carry):
        put(ybuf, g, loads_at(g) - product(g))
        return carry

    lax.fori_loop(0, 4, first_outer, 0)
    lax.fori_loop(4, 8, first_inner, 0)
    _, coeff = gather(0, fold(image_terms(0)))
    wait_halo_sent(0)
    side = spread_side(coeff)
    part = jnp.zeros((8, width), F32)
    for g in range(8):
        value = assembled(g, 0)
        put(res, g, value)
        value = value - correct(g, side)
        put(dire, g, value)
        part = part + weight(g) * rows8(value * value)
    gamma = None

    for iteration in range(ITERS):
        par = (iteration + 1) % 2
        last = iteration + 1 == ITERS
        load_side(dire)

        def outer(step, carry):
            f = (step + 2) % 4
            value = product(f)
            put(ybuf, f, value)
            start_halo(f, par)
            return carry + rows8(value * at(dire, f))

        def inner(g, carry):
            value = product(g)
            put(ybuf, g, value)
            return carry + rows8(value * at(dire, g))

        curv = lax.fori_loop(0, 4, outer, jnp.zeros((8, width), F32))
        curv = lax.fori_loop(4, 8, inner, curv)
        curv = jnp.sum(curv, axis=0, keepdims=True)
        message = jnp.where(row_ids == PAD - 2, curv, fold(image_terms(par)))
        if gamma is None:
            message = jnp.where(row_ids == PAD - 1, jnp.sum(part, axis=0, keepdims=True), message)
        sums, coeff_image = gather(par, message)
        wait_halo_sent(par)
        if gamma is None:
            gamma = sums[PAD - 1:PAD]
        length = gamma / sums[PAD - 2:PAD - 1]
        coeff = coeff - length * coeff_image
        side = spread_side(coeff)
        part = jnp.zeros((8, width), F32)
        for g in range(8):
            value = at(res, g) - length * assembled(g, par)
            if not last:
                put(res, g, value)
            value = value - correct(g, side)
            put(proj, g, value)
            if not last:
                part = part + weight(g) * rows8(value * value)
        if last:
            for b in range(nblk):
                s = inv_ref[b]
                mult_out[b] = mult[s] + length * dire[s]
                proj_out[b] = proj[s]
        else:
            def step_multipliers():
                for g in range(8):
                    put(mult, g, at(mult, g) + length * at(dire, g))

            following = total(part, step_multipliers)
            ratio = following / gamma
            gamma = following
            for g in range(8):
                put(dire, g, at(proj, g) + ratio * at(dire, g))


def solution(mesh):
    nc, ns = mesh.shape["cluster"], mesh.shape["sub"]
    devices = nc * ns

    def on_device(dual_operators, local_loads, modes, coarse_matrix, coarse_loads, slot_block):
        parts, order, loads = local_loads.shape
        nmode = modes.shape[1]
        slots = slot_block[0]
        nblk = slots.shape[0]
        face = nblk // 8
        blk = order * parts // nblk
        unit = parts * PAD
        positions = jnp.arange(nblk, dtype=jnp.int32)
        inverse = jnp.sum(
            positions[:, None] * (slots[:, None] == positions[None, :]).astype(jnp.int32), axis=0)
        vmem = pl.BlockSpec(memory_space=pltpu.VMEM)
        smem = pl.BlockSpec(memory_space=pltpu.SMEM)
        anym = pl.BlockSpec(memory_space=pl.ANY)
        vec = pltpu.VMEM((nblk, blk, loads), F32)
        dma = pltpu.SemaphoreType.DMA
        out = jax.ShapeDtypeStruct((nblk, blk, loads), F32)
        mult, proj = pl.pallas_call(
            functools.partial(kernel, nc, ns, parts, face),
            out_shape=(out, out),
            in_specs=[smem, smem, anym, anym, vmem, vmem, vmem],
            out_specs=(vmem, vmem),
            scratch_shapes=[
                pltpu.VMEM((nblk, blk, order), BF16),
                vec, vec, vec, vec, vec,
                pltpu.VMEM((8, face * blk, 2 * LANES), BF16),
                pltpu.VMEM((order, parts * loads), BF16),
                pltpu.VMEM((2, 4, face, blk, loads), F32),
                pltpu.VMEM((nblk, PAD, blk), F32),
                pltpu.VMEM((nblk, unit, blk), F32),
                pltpu.VMEM((4, face, unit, blk), F32),
                pltpu.VMEM((8, 2 * unit, face * blk), BF16),
                pltpu.VMEM((5, unit, coarse_matrix.shape[1]), F32),
                pltpu.VMEM((10 * unit, devices * unit), BF16),
                pltpu.VMEM((2, nc, ns, unit, loads), F32),
                pltpu.VMEM((nc, 8, loads), F32),
                pltpu.VMEM((ns, 8, loads), F32),
                dma((8,)), dma(()),
                dma((4,)), dma((2, 4)), dma((4,)), dma((4,)), dma((4,)), dma((4,)),
                dma((nc,)), dma((2, nc)), dma((ns,)), dma((2, ns)), dma((nc,)), dma((ns,)),
            ],
            compiler_params=pltpu.CompilerParams(
                collective_id=0, has_side_effects=True, vmem_limit_bytes=56 * 1024 * 1024),
            cost_estimate=pl.CostEstimate(
                flops=8 * parts * order * order * loads, bytes_accessed=24 * 1024 * 1024, transcendentals=0),
        )(slot_block, inverse, dual_operators.reshape(nblk, blk, order),
          local_loads.reshape(nblk, blk, loads), modes, coarse_matrix, coarse_loads)
        return mult.reshape(local_loads.shape), proj.reshape(local_loads.shape)

    return jax.shard_map(
        on_device,
        mesh=mesh,
        in_specs=(
            P(("cluster", "sub"), None, None),
            P(("cluster", "sub"), None, None),
            P(("cluster", "sub"), None, None),
            P(("cluster", "sub"), None),
            P(),
            P(("cluster", "sub"), None),
        ),
        out_specs=(P(("cluster", "sub"), None, None), P(("cluster", "sub"), None, None)),
        check_vma=False,
    )
```

```python
import functools

import jax
import jax.numpy as jnp
from jax import lax
from jax.experimental import pallas as pl
from jax.experimental.pallas import tpu as pltpu
from jax.sharding import PartitionSpec as P

ITERS = 3
PAD = 8
LANES = 128
MESH = pl.DeviceIdType.MESH
F32, BF16 = jnp.float32, jnp.bfloat16


def split(x):
    high = x.astype(BF16)
    return high, (x - high.astype(F32)).astype(BF16)


def rows8(x):
    return jnp.sum(x.reshape(-1, 8, x.shape[-1]), axis=0)


def kernel(
    nc, ns, parts, face,
    slot_ref, inv_ref, ops_hbm, loads_hbm, modes_ref, cmat_ref, cload_ref,
    out_ref,
    ops, ybuf, res, proj, dire, mult, emat, vb, halo, mraw, mslot, mfetch, mhl, call, cpad, hall, gz, gs,
    ops_sem, loads_sem, halo_send, halo_recv, m_send, m_recv, c_send, c_recv,
    zsend, zrecv, ssend, srecv, gzrecv, gsrecv,
):
    c, i = lax.axis_index("cluster"), lax.axis_index("sub")
    nblk = 8 * face
    per = nblk // parts
    blk = ybuf.shape[1]
    frows = face * blk
    unit = parts * PAD
    width = ybuf.shape[-1]

    nmode = modes_ref.shape[0]
    ops_copies = [
        pltpu.make_async_copy(
            ops_hbm.at[pl.ds(k * face, face)], ops.at[pl.ds(k * face, face)], ops_sem.at[k])
        for k in range(8)]
    for copy in ops_copies:
        copy.start()
    loads_copy = pltpu.make_async_copy(loads_hbm, proj, loads_sem)
    loads_copy.start()

    barrier = pltpu.get_barrier_semaphore()
    for k in range(1, nc):
        pl.semaphore_signal(barrier, inc=1, device_id=(lax.rem(c + k, nc), i), device_id_type=MESH)
    for k in range(1, ns):
        pl.semaphore_signal(barrier, inc=1, device_id=(c, lax.rem(i + k, ns)), device_id_type=MESH)

    mraw[...] = jnp.zeros_like(mraw)
    for b in range(nblk):
        t, r = b // per, b % per
        for m in range(nmode):
            mraw[b, m:m + 1, :] = modes_ref[m, t:t + 1, r * blk:(r + 1) * blk]
    for j in range(nblk):
        b = slot_ref[0, j]
        piece = mraw[b]
        block = jnp.broadcast_to(b, piece.shape)
        for own in range(parts):
            mine = (block >= own * per) & (block < (own + 1) * per)
            mslot[j, own * PAD:(own + 1) * PAD, :] = jnp.where(mine, piece, 0.0)
    call[0] = jnp.zeros(call.shape[1:], F32)
    for t in range(parts):
        call[0, t * PAD:t * PAD + nmode, :] = cmat_ref[t * nmode:(t + 1) * nmode, :]

    def partner(f):
        axis, sign = f // 2, 2 * (f % 2) - 1
        tc, ti = c + axis * sign, i + (1 - axis) * sign
        there = (tc >= 0) & (tc < nc) & (ti >= 0) & (ti < ns)
        return there, (tc, ti), axis * 2 + 1 - f % 2

    def halo_copy(f, landing, par):
        _, device, _ = partner(f)
        return pltpu.make_async_remote_copy(
            src_ref=ybuf.at[pl.ds(f * face, face)], dst_ref=halo.at[par, landing],
            send_sem=halo_send.at[f], recv_sem=halo_recv.at[par, landing],
            device_id=device, device_id_type=MESH)

    def mode_copy(f, landing):
        _, device, _ = partner(f)
        return pltpu.make_async_remote_copy(
            src_ref=mslot.at[pl.ds(f * face, face)], dst_ref=mfetch.at[landing],
            send_sem=m_send.at[f], recv_sem=m_recv.at[landing],
            device_id=device, device_id_type=MESH)

    def coarse_copy(f, landing):
        _, device, _ = partner(f)
        return pltpu.make_async_remote_copy(
            src_ref=call.at[0], dst_ref=call.at[landing + 1],
            send_sem=c_send.at[f], recv_sem=c_recv.at[landing],
            device_id=device, device_id_type=MESH)

    pl.semaphore_wait(barrier, nc + ns - 2)
    for f in range(4):
        there, _, landing = partner(f)

        @pl.when(there)
        def _():
            mode_copy(f, landing).start()
            coarse_copy(f, landing).start()

        @pl.when(jnp.logical_not(there))
        def _():
            halo[0, f] = jnp.zeros(halo.shape[2:], F32)
            halo[1, f] = jnp.zeros(halo.shape[2:], F32)
            mfetch[f] = jnp.zeros(mfetch.shape[1:], F32)
            call[f + 1] = jnp.zeros(call.shape[1:], F32)

    for g in range(8):
        for k in range(face):
            j = g * face + k
            own = mslot[j]
            if g == 6:
                own = own - mslot[j + face]
            if g == 7:
                own = own - mslot[j - face]
            high, low = split(own)
            mhl[g, 0:unit, k * blk:(k + 1) * blk] = high
            mhl[g, unit:2 * unit, k * blk:(k + 1) * blk] = low

    for f in range(4):
        there, _, _ = partner(f)

        @pl.when(there)
        def _():
            mode_copy(f, f).wait_recv()
            coarse_copy(f, f).wait_recv()
            mode_copy(f, f).wait_send()
            coarse_copy(f, f).wait_send()

    for g in range(8):
        for k in range(face):
            j = g * face + k
            own = mslot[j]
            if g == 6:
                own = own - mslot[j + face]
            if g == 7:
                own = own - mslot[j - face]
            pieces = [own]
            if g < 4:
                if g > 0:
                    pieces.append(jnp.zeros((g * unit, blk), F32))
                pieces.append(-mfetch[g, k])
            used = sum(x.shape[0] for x in pieces)
            pieces.append(jnp.zeros((LANES - used, blk), F32))
            high, low = split(jnp.concatenate(pieces, axis=0).T)
            emat[g, k * blk:(k + 1) * blk, 0:LANES] = high
            emat[g, k * blk:(k + 1) * blk, LANES:] = low

    highest = lax.Precision.HIGHEST
    cfull = call[...].reshape(5 * unit, call.shape[-1])
    first = jnp.dot(cfull, cload_ref[...], precision=highest, preferred_element_type=F32)
    columns = call.shape[-1]
    chunk = nmode * LANES // 2
    if columns % chunk:
        chunk = columns
    padded = chunk // nmode * PAD
    place_rows = lax.broadcasted_iota(jnp.int32, (chunk, padded), 0)
    place_cols = lax.broadcasted_iota(jnp.int32, (chunk, padded), 1)
    group, mode = place_cols >> 3, place_cols & (PAD - 1)
    place = jnp.where((place_rows == group * nmode + mode) & (mode < nmode), 1.0, 0.0).astype(F32)
    for k in range(columns // chunk):
        high, low = split(jnp.dot(
            cfull[:, k * chunk:(k + 1) * chunk], place, precision=highest, preferred_element_type=F32))
        cpad[0:5 * unit, k * padded:(k + 1) * padded] = high
        cpad[5 * unit:10 * unit, k * padded:(k + 1) * padded] = low

    def coarse(terms):
        high, low = split(terms)
        both = jnp.dot(cpad[...], jnp.concatenate([high, low], axis=1), preferred_element_type=F32)
        top = 5 * unit
        return both[:top, :width] + (both[:top, width:] + both[top:, :width])

    def spread_side(coeff):
        high, low = split(jnp.concatenate(
            [coeff, jnp.zeros((LANES - coeff.shape[0], coeff.shape[1]), F32)], axis=0))
        top = jnp.concatenate([high, low], axis=1)
        bottom = jnp.concatenate([high, jnp.zeros_like(low)], axis=1)
        return jnp.concatenate([top, bottom], axis=0)

    def correct(g, side):
        both = jnp.dot(emat[g], side, preferred_element_type=F32)
        width = both.shape[1] // 2
        return both[:, :width] + both[:, width:]

    def at(ref, g):
        return ref[pl.ds(g * face, face)].reshape(frows, ref.shape[-1])

    def put(ref, g, value):
        ref[pl.ds(g * face, face)] = value.reshape(face, blk, value.shape[-1])

    def load_side(source):
        for b in range(nblk):
            t, r = b // per, b % per
            vb[r * blk:(r + 1) * blk, t * width:(t + 1) * width] = source[inv_ref[b]].astype(BF16)

    def product(g):
        pieces, blocks = [], []
        for k in range(face):
            b = slot_ref[0, g * face + k]
            pieces.append(ops[b])
            blocks.append(jnp.broadcast_to(b, (blk, width)))
        rows = jnp.concatenate(pieces, axis=0)
        half = rows.shape[1] // 2
        wide = (jnp.dot(rows[:, :half], vb[:half], preferred_element_type=F32)
                + jnp.dot(rows[:, half:], vb[half:], preferred_element_type=F32))
        block = jnp.concatenate(blocks, axis=0)
        value = wide[:, :width]
        for t in range(1, parts):
            value = jnp.where(block >= t * per, wide[:, t * width:(t + 1) * width], value)
        return value

    def start_halo(f, par):
        there, _, landing = partner(f)

        @pl.when(there)
        def _():
            halo_copy(f, landing, par).start()

    def wait_halo(f, par):
        there, _, _ = partner(f)

        @pl.when(there)
        def _():
            halo_copy(f, f, par).wait_recv()

    def wait_halo_sent(par):
        for f in range(4):
            there, _, _ = partner(f)

            @pl.when(there)
            def _():
                halo_copy(f, f, par).wait_send()

    def assembled(g, par):
        mine = at(ybuf, g)
        if g < 4:
            return mine - halo[par, g].reshape(frows, width)
        if g < 6:
            return mine
        return mine - at(ybuf, 13 - g)

    def terms_of(g, value):
        high, low = split(value)
        return jnp.dot(mhl[g], jnp.concatenate([high, low], axis=1), preferred_element_type=F32)

    def image_terms(par):
        terms = lax.fori_loop(
            0, 8, lambda g, carry: carry + terms_of(g, at(ybuf, g)),
            jnp.zeros((2 * unit, 2 * width), F32))
        for f in range(4):
            wait_halo(f, par)
            terms = terms - terms_of(f, halo[par, f].reshape(frows, width))
        return terms

    def fold(both):
        return both[:unit, :width] + (both[:unit, width:] + both[unit:, :width])

    def weight(g):
        if g < 4:
            there, _, _ = partner(g)
            return jnp.where(there, 0.5, 1.0).astype(F32)
        return 1.0 if g < 6 else 0.5

    def gather(par, terms):
        hall[par, c, i] = terms
        zs, ss = [], []
        for k in range(1, nc):
            zs.append(pltpu.make_async_remote_copy(
                src_ref=hall.at[par, c, i], dst_ref=hall.at[par, c, i],
                send_sem=zsend.at[k], recv_sem=zrecv.at[par, c],
                device_id=(lax.rem(c + k, nc), i), device_id_type=MESH))
        for copy in zs:
            copy.start()
        for k in range(1, nc):
            peer = lax.rem(c + k, nc)
            pltpu.make_async_remote_copy(
                src_ref=hall.at[par, peer, i], dst_ref=hall.at[par, peer, i],
                send_sem=zsend.at[k], recv_sem=zrecv.at[par, peer],
                device_id=(peer, i), device_id_type=MESH).wait_recv()
        for k in range(1, ns):
            ss.append(pltpu.make_async_remote_copy(
                src_ref=hall.at[par, :, i], dst_ref=hall.at[par, :, i],
                send_sem=ssend.at[k], recv_sem=srecv.at[par, i],
                device_id=(c, lax.rem(i + k, ns)), device_id_type=MESH))
        for copy in ss:
            copy.start()
        for k in range(1, ns):
            peer = lax.rem(i + k, ns)
            pltpu.make_async_remote_copy(
                src_ref=hall.at[par, :, peer], dst_ref=hall.at[par, :, peer],
                send_sem=ssend.at[k], recv_sem=srecv.at[par, peer],
                device_id=(c, peer), device_id_type=MESH).wait_recv()
        for copy in zs + ss:
            copy.wait_send()
        whole = hall[par].reshape(nc * ns, unit, width)
        return jnp.sum(whole, axis=0), coarse(whole.reshape(nc * ns * unit, width))

    def total(value, meanwhile):
        gz[c] = value
        zs, ss = [], []
        for k in range(1, nc):
            zs.append(pltpu.make_async_remote_copy(
                src_ref=gz.at[c], dst_ref=gz.at[c], send_sem=zsend.at[k], recv_sem=gzrecv.at[c],
                device_id=(lax.rem(c + k, nc), i), device_id_type=MESH))
        for copy in zs:
            copy.start()
        meanwhile()
        for k in range(1, nc):
            peer = lax.rem(c + k, nc)
            pltpu.make_async_remote_copy(
                src_ref=gz.at[peer], dst_ref=gz.at[peer], send_sem=zsend.at[k], recv_sem=gzrecv.at[peer],
                device_id=(peer, i), device_id_type=MESH).wait_recv()
        gs[i] = jnp.sum(gz[...], axis=0)
        for k in range(1, ns):
            ss.append(pltpu.make_async_remote_copy(
                src_ref=gs.at[i], dst_ref=gs.at[i], send_sem=ssend.at[k], recv_sem=gsrecv.at[i],
                device_id=(c, lax.rem(i + k, ns)), device_id_type=MESH))
        for copy in ss:
            copy.start()
        for k in range(1, ns):
            peer = lax.rem(i + k, ns)
            pltpu.make_async_remote_copy(
                src_ref=gs.at[peer], dst_ref=gs.at[peer], send_sem=ssend.at[k], recv_sem=gsrecv.at[peer],
                device_id=(c, peer), device_id_type=MESH).wait_recv()
        for copy in zs + ss:
            copy.wait_send()
        return jnp.sum(jnp.sum(gs[...], axis=0), axis=0, keepdims=True)

    row_ids = lax.broadcasted_iota(jnp.int32, (unit, width), 0)

    side = spread_side(first)
    for g in range(8):
        put(mult, g, correct(g, side))
    load_side(mult)
    loads_copy.wait()
    for copy in ops_copies:
        copy.wait()

    def loads_at(g):
        return jnp.concatenate([proj[slot_ref[0, g * face + k]] for k in range(face)], axis=0)

    def first_outer(step, carry):
        f = (step + 2) % 4
        put(ybuf, f, loads_at(f) - product(f))
        start_halo(f, 0)
        return carry

    def first_inner(g, carry):
        put(ybuf, g, loads_at(g) - product(g))
        return carry

    lax.fori_loop(0, 4, first_outer, 0)
    lax.fori_loop(4, 8, first_inner, 0)
    _, coeff = gather(0, fold(image_terms(0)))
    wait_halo_sent(0)
    side = spread_side(coeff)
    part = jnp.zeros((8, width), F32)
    for g in range(8):
        value = assembled(g, 0)
        put(res, g, value)
        value = value - correct(g, side)
        put(dire, g, value)
        part = part + weight(g) * rows8(value * value)
    gamma = None

    for iteration in range(ITERS):
        par = (iteration + 1) % 2
        last = iteration + 1 == ITERS
        load_side(dire)

        def outer(step, carry):
            f = (step + 2) % 4
            value = product(f)
            put(ybuf, f, value)
            start_halo(f, par)
            return carry + rows8(value * at(dire, f))

        def inner(g, carry):
            value = product(g)
            put(ybuf, g, value)
            return carry + rows8(value * at(dire, g))

        curv = lax.fori_loop(0, 4, outer, jnp.zeros((8, width), F32))
        curv = lax.fori_loop(4, 8, inner, curv)
        curv = jnp.sum(curv, axis=0, keepdims=True)
        message = jnp.where(row_ids == PAD - 2, curv, fold(image_terms(par)))
        if gamma is None:
            message = jnp.where(row_ids == PAD - 1, jnp.sum(part, axis=0, keepdims=True), message)
        sums, coeff_image = gather(par, message)
        wait_halo_sent(par)
        if gamma is None:
            gamma = sums[PAD - 1:PAD]
        length = gamma / sums[PAD - 2:PAD - 1]
        coeff = coeff - length * coeff_image
        side = spread_side(coeff)
        part = jnp.zeros((8, width), F32)
        for g in range(8):
            value = at(res, g) - length * assembled(g, par)
            if not last:
                put(res, g, value)
            value = value - correct(g, side)
            put(proj, g, value)
            if not last:
                part = part + weight(g) * rows8(value * value)
        if last:
            for b in range(nblk):
                s = inv_ref[b]
                out_ref[0, b] = mult[s] + length * dire[s]
                out_ref[1, b] = proj[s]
        else:
            def step_multipliers():
                for g in range(8):
                    put(mult, g, at(mult, g) + length * at(dire, g))

            following = total(part, step_multipliers)
            ratio = following / gamma
            gamma = following
            for g in range(8):
                put(dire, g, at(proj, g) + ratio * at(dire, g))


def solution(mesh):
    nc, ns = mesh.shape["cluster"], mesh.shape["sub"]
    devices = nc * ns

    def on_device(dual_operators, local_loads, modes, coarse_matrix, coarse_loads, slot_block):
        parts, order, loads = local_loads.shape
        nmode = modes.shape[1]
        slots = slot_block[0]
        nblk = slots.shape[0]
        face = nblk // 8
        blk = order * parts // nblk
        unit = parts * PAD
        positions = jnp.arange(nblk, dtype=jnp.int32)
        inverse = jnp.sum(
            positions[:, None] * (slots[:, None] == positions[None, :]).astype(jnp.int32), axis=0)
        vmem = pl.BlockSpec(memory_space=pltpu.VMEM)
        smem = pl.BlockSpec(memory_space=pltpu.SMEM)
        anym = pl.BlockSpec(memory_space=pl.ANY)
        vec = pltpu.VMEM((nblk, blk, loads), F32)
        dma = pltpu.SemaphoreType.DMA
        out = jax.ShapeDtypeStruct((2, nblk, blk, loads), F32)
        both = pl.pallas_call(
            functools.partial(kernel, nc, ns, parts, face),
            out_shape=out,
            in_specs=[smem, smem, anym, anym, vmem, vmem, vmem],
            out_specs=vmem,
            scratch_shapes=[
                pltpu.VMEM((nblk, blk, order), BF16),
                vec, vec, vec, vec, vec,
                pltpu.VMEM((8, face * blk, 2 * LANES), BF16),
                pltpu.VMEM((order, parts * loads), BF16),
                pltpu.VMEM((2, 4, face, blk, loads), F32),
                pltpu.VMEM((nblk, PAD, blk), F32),
                pltpu.VMEM((nblk, unit, blk), F32),
                pltpu.VMEM((4, face, unit, blk), F32),
                pltpu.VMEM((8, 2 * unit, face * blk), BF16),
                pltpu.VMEM((5, unit, coarse_matrix.shape[1]), F32),
                pltpu.VMEM((10 * unit, devices * unit), BF16),
                pltpu.VMEM((2, nc, ns, unit, loads), F32),
                pltpu.VMEM((nc, 8, loads), F32),
                pltpu.VMEM((ns, 8, loads), F32),
                dma((8,)), dma(()),
                dma((4,)), dma((2, 4)), dma((4,)), dma((4,)), dma((4,)), dma((4,)),
                dma((nc,)), dma((2, nc)), dma((ns,)), dma((2, ns)), dma((nc,)), dma((ns,)),
            ],
            compiler_params=pltpu.CompilerParams(
                collective_id=0, has_side_effects=True, vmem_limit_bytes=56 * 1024 * 1024),
            cost_estimate=pl.CostEstimate(
                flops=8 * parts * order * order * loads, bytes_accessed=24 * 1024 * 1024, transcendentals=0),
        )(slot_block, inverse, dual_operators.reshape(nblk, blk, order),
          local_loads.reshape(nblk, blk, loads), modes.transpose(1, 0, 2), coarse_matrix, coarse_loads)
        return both[0].reshape(local_loads.shape), both[1].reshape(local_loads.shape)

    return jax.shard_map(
        on_device,
        mesh=mesh,
        in_specs=(
            P(("cluster", "sub"), None, None),
            P(("cluster", "sub"), None, None),
            P(("cluster", "sub"), None, None),
            P(("cluster", "sub"), None),
            P(),
            P(("cluster", "sub"), None),
        ),
        out_specs=(P(("cluster", "sub"), None, None), P(("cluster", "sub"), None, None)),
        check_vma=False,
    )
```

```python
import functools

import jax
import jax.numpy as jnp
from jax import lax
from jax.experimental import pallas as pl
from jax.experimental.pallas import tpu as pltpu
from jax.sharding import PartitionSpec as P

ITERS = 3
PAD = 8
LANES = 128
MESH = pl.DeviceIdType.MESH
F32, BF16 = jnp.float32, jnp.bfloat16


def split(x):
    high = x.astype(BF16)
    return high, (x - high.astype(F32)).astype(BF16)


def rows8(x):
    return jnp.sum(x.reshape(-1, 8, x.shape[-1]), axis=0)


def kernel(
    nc, ns, parts, face,
    slot_ref, inv_ref, ops_hbm, loads_hbm, modes_ref, cmat_ref, cload_ref,
    out_ref,
    ops, ybuf, res, proj, dire, mult, emat, vb, halo, mraw, mslot, mfetch, mhl, call, cpad, hall, gz, gs,
    ops_sem, loads_sem, halo_send, halo_recv, m_send, m_recv, c_send, c_recv,
    zsend, zrecv, ssend, srecv, gzrecv, gsrecv,
):
    c, i = lax.axis_index("cluster"), lax.axis_index("sub")
    nblk = 8 * face
    per = nblk // parts
    blk = ybuf.shape[1]
    frows = face * blk
    unit = parts * PAD
    width = ybuf.shape[-1]

    nmode = modes_ref.shape[0]
    ops_copies = [
        pltpu.make_async_copy(
            ops_hbm.at[pl.ds(k * face, face)], ops.at[pl.ds(k * face, face)], ops_sem.at[k])
        for k in range(8)]
    for copy in ops_copies:
        copy.start()
    loads_copy = pltpu.make_async_copy(loads_hbm, proj, loads_sem)
    loads_copy.start()

    barrier = pltpu.get_barrier_semaphore()
    for k in range(1, nc):
        pl.semaphore_signal(barrier, inc=1, device_id=(lax.rem(c + k, nc), i), device_id_type=MESH)
    for k in range(1, ns):
        pl.semaphore_signal(barrier, inc=1, device_id=(c, lax.rem(i + k, ns)), device_id_type=MESH)

    mraw[...] = jnp.zeros_like(mraw)
    for b in range(nblk):
        t, r = b // per, b % per
        for m in range(nmode):
            mraw[b, m:m + 1, :] = modes_ref[m, t:t + 1, r * blk:(r + 1) * blk]
    for j in range(nblk):
        b = slot_ref[0, j]
        piece = mraw[b]
        block = jnp.broadcast_to(b, piece.shape)
        for own in range(parts):
            mine = (block >= own * per) & (block < (own + 1) * per)
            mslot[j, own * PAD:(own + 1) * PAD, :] = jnp.where(mine, piece, 0.0)
    call[0] = jnp.zeros(call.shape[1:], F32)
    for t in range(parts):
        call[0, t * PAD:t * PAD + nmode, :] = cmat_ref[t * nmode:(t + 1) * nmode, :]

    def partner(f):
        axis, sign = f // 2, 2 * (f % 2) - 1
        tc, ti = c + axis * sign, i + (1 - axis) * sign
        there = (tc >= 0) & (tc < nc) & (ti >= 0) & (ti < ns)
        return there, (tc, ti), axis * 2 + 1 - f % 2

    def halo_copy(f, landing, par):
        _, device, _ = partner(f)
        return pltpu.make_async_remote_copy(
            src_ref=ybuf.at[pl.ds(f * face, face)], dst_ref=halo.at[par, landing],
            send_sem=halo_send.at[f], recv_sem=halo_recv.at[par, landing],
            device_id=device, device_id_type=MESH)

    def mode_copy(f, landing):
        _, device, _ = partner(f)
        return pltpu.make_async_remote_copy(
            src_ref=mslot.at[pl.ds(f * face, face)], dst_ref=mfetch.at[landing],
            send_sem=m_send.at[f], recv_sem=m_recv.at[landing],
            device_id=device, device_id_type=MESH)

    def coarse_copy(f, landing):
        _, device, _ = partner(f)
        return pltpu.make_async_remote_copy(
            src_ref=call.at[0], dst_ref=call.at[landing + 1],
            send_sem=c_send.at[f], recv_sem=c_recv.at[landing],
            device_id=device, device_id_type=MESH)

    pl.semaphore_wait(barrier, nc + ns - 2)
    for f in range(4):
        there, _, landing = partner(f)

        @pl.when(there)
        def _():
            mode_copy(f, landing).start()
            coarse_copy(f, landing).start()

        @pl.when(jnp.logical_not(there))
        def _():
            halo[0, f] = jnp.zeros(halo.shape[2:], F32)
            halo[1, f] = jnp.zeros(halo.shape[2:], F32)
            mfetch[f] = jnp.zeros(mfetch.shape[1:], F32)
            call[f + 1] = jnp.zeros(call.shape[1:], F32)

    for g in range(8):
        for k in range(face):
            j = g * face + k
            own = mslot[j]
            if g == 6:
                own = own - mslot[j + face]
            if g == 7:
                own = own - mslot[j - face]
            high, low = split(own)
            mhl[g, 0:unit, k * blk:(k + 1) * blk] = high
            mhl[g, unit:2 * unit, k * blk:(k + 1) * blk] = low

    for f in range(4):
        there, _, _ = partner(f)

        @pl.when(there)
        def _():
            mode_copy(f, f).wait_recv()
            coarse_copy(f, f).wait_recv()
            mode_copy(f, f).wait_send()
            coarse_copy(f, f).wait_send()

    for g in range(8):
        for k in range(face):
            j = g * face + k
            own = mslot[j]
            if g == 6:
                own = own - mslot[j + face]
            if g == 7:
                own = own - mslot[j - face]
            pieces = [own]
            if g < 4:
                if g > 0:
                    pieces.append(jnp.zeros((g * unit, blk), F32))
                pieces.append(-mfetch[g, k])
            used = sum(x.shape[0] for x in pieces)
            pieces.append(jnp.zeros((LANES - used, blk), F32))
            high, low = split(jnp.concatenate(pieces, axis=0).T)
            emat[g, k * blk:(k + 1) * blk, 0:LANES] = high
            emat[g, k * blk:(k + 1) * blk, LANES:] = low

    highest = lax.Precision.HIGHEST
    cfull = call[...].reshape(5 * unit, call.shape[-1])
    first = jnp.dot(cfull, cload_ref[...], precision=highest, preferred_element_type=F32)
    def coarse(terms):
        high, low = split(terms)
        both = jnp.dot(cpad[...], jnp.concatenate([high, low], axis=1), preferred_element_type=F32)
        top = 5 * unit
        return both[:top, :width] + (both[:top, width:] + both[top:, :width])

    def spread_side(coeff):
        high, low = split(jnp.concatenate(
            [coeff, jnp.zeros((LANES - coeff.shape[0], coeff.shape[1]), F32)], axis=0))
        top = jnp.concatenate([high, low], axis=1)
        bottom = jnp.concatenate([high, jnp.zeros_like(low)], axis=1)
        return jnp.concatenate([top, bottom], axis=0)

    def correct(g, side):
        both = jnp.dot(emat[g], side, preferred_element_type=F32)
        width = both.shape[1] // 2
        return both[:, :width] + both[:, width:]

    def at(ref, g):
        return ref[pl.ds(g * face, face)].reshape(frows, ref.shape[-1])

    def put(ref, g, value):
        ref[pl.ds(g * face, face)] = value.reshape(face, blk, value.shape[-1])

    def load_side(source):
        for b in range(nblk):
            t, r = b // per, b % per
            vb[r * blk:(r + 1) * blk, t * width:(t + 1) * width] = source[inv_ref[b]].astype(BF16)

    def product(g):
        pieces, blocks = [], []
        for k in range(face):
            b = slot_ref[0, g * face + k]
            pieces.append(ops[b])
            blocks.append(jnp.broadcast_to(b, (blk, width)))
        rows = jnp.concatenate(pieces, axis=0)
        half = rows.shape[1] // 2
        wide = (jnp.dot(rows[:, :half], vb[:half], preferred_element_type=F32)
                + jnp.dot(rows[:, half:], vb[half:], preferred_element_type=F32))
        block = jnp.concatenate(blocks, axis=0)
        value = wide[:, :width]
        for t in range(1, parts):
            value = jnp.where(block >= t * per, wide[:, t * width:(t + 1) * width], value)
        return value

    def start_halo(f, par):
        there, _, landing = partner(f)

        @pl.when(there)
        def _():
            halo_copy(f, landing, par).start()

    def wait_halo(f, par):
        there, _, _ = partner(f)

        @pl.when(there)
        def _():
            halo_copy(f, f, par).wait_recv()

    def wait_halo_sent(par):
        for f in range(4):
            there, _, _ = partner(f)

            @pl.when(there)
            def _():
                halo_copy(f, f, par).wait_send()

    def assembled(g, par):
        mine = at(ybuf, g)
        if g < 4:
            return mine - halo[par, g].reshape(frows, width)
        if g < 6:
            return mine
        return mine - at(ybuf, 13 - g)

    def terms_of(g, value):
        high, low = split(value)
        return jnp.dot(mhl[g], jnp.concatenate([high, low], axis=1), preferred_element_type=F32)

    def image_terms(par):
        terms = lax.fori_loop(
            0, 8, lambda g, carry: carry + terms_of(g, at(ybuf, g)),
            jnp.zeros((2 * unit, 2 * width), F32))
        for f in range(4):
            wait_halo(f, par)
            terms = terms - terms_of(f, halo[par, f].reshape(frows, width))
        return terms

    def fold(both):
        return both[:unit, :width] + (both[:unit, width:] + both[unit:, :width])

    def weight(g):
        if g < 4:
            there, _, _ = partner(g)
            return jnp.where(there, 0.5, 1.0).astype(F32)
        return 1.0 if g < 6 else 0.5

    def gather(par, terms):
        hall[par, c, i] = terms
        zs, ss = [], []
        for k in range(1, nc):
            zs.append(pltpu.make_async_remote_copy(
                src_ref=hall.at[par, c, i], dst_ref=hall.at[par, c, i],
                send_sem=zsend.at[k], recv_sem=zrecv.at[par, c],
                device_id=(lax.rem(c + k, nc), i), device_id_type=MESH))
        for copy in zs:
            copy.start()
        for k in range(1, nc):
            peer = lax.rem(c + k, nc)
            pltpu.make_async_remote_copy(
                src_ref=hall.at[par, peer, i], dst_ref=hall.at[par, peer, i],
                send_sem=zsend.at[k], recv_sem=zrecv.at[par, peer],
                device_id=(peer, i), device_id_type=MESH).wait_recv()
        for k in range(1, ns):
            ss.append(pltpu.make_async_remote_copy(
                src_ref=hall.at[par, :, i], dst_ref=hall.at[par, :, i],
                send_sem=ssend.at[k], recv_sem=srecv.at[par, i],
                device_id=(c, lax.rem(i + k, ns)), device_id_type=MESH))
        for copy in ss:
            copy.start()
        for k in range(1, ns):
            peer = lax.rem(i + k, ns)
            pltpu.make_async_remote_copy(
                src_ref=hall.at[par, :, peer], dst_ref=hall.at[par, :, peer],
                send_sem=ssend.at[k], recv_sem=srecv.at[par, peer],
                device_id=(c, peer), device_id_type=MESH).wait_recv()
        for copy in zs + ss:
            copy.wait_send()
        whole = hall[par].reshape(nc * ns, unit, width)
        return jnp.sum(whole, axis=0), coarse(whole.reshape(nc * ns * unit, width))

    def total(value, meanwhile):
        gz[c] = value
        zs, ss = [], []
        for k in range(1, nc):
            zs.append(pltpu.make_async_remote_copy(
                src_ref=gz.at[c], dst_ref=gz.at[c], send_sem=zsend.at[k], recv_sem=gzrecv.at[c],
                device_id=(lax.rem(c + k, nc), i), device_id_type=MESH))
        for copy in zs:
            copy.start()
        meanwhile()
        for k in range(1, nc):
            peer = lax.rem(c + k, nc)
            pltpu.make_async_remote_copy(
                src_ref=gz.at[peer], dst_ref=gz.at[peer], send_sem=zsend.at[k], recv_sem=gzrecv.at[peer],
                device_id=(peer, i), device_id_type=MESH).wait_recv()
        gs[i] = jnp.sum(gz[...], axis=0)
        for k in range(1, ns):
            ss.append(pltpu.make_async_remote_copy(
                src_ref=gs.at[i], dst_ref=gs.at[i], send_sem=ssend.at[k], recv_sem=gsrecv.at[i],
                device_id=(c, lax.rem(i + k, ns)), device_id_type=MESH))
        for copy in ss:
            copy.start()
        for k in range(1, ns):
            peer = lax.rem(i + k, ns)
            pltpu.make_async_remote_copy(
                src_ref=gs.at[peer], dst_ref=gs.at[peer], send_sem=ssend.at[k], recv_sem=gsrecv.at[peer],
                device_id=(c, peer), device_id_type=MESH).wait_recv()
        for copy in zs + ss:
            copy.wait_send()
        return jnp.sum(jnp.sum(gs[...], axis=0), axis=0, keepdims=True)

    row_ids = lax.broadcasted_iota(jnp.int32, (unit, width), 0)

    side = spread_side(first)
    for g in range(8):
        put(mult, g, correct(g, side))
    load_side(mult)
    loads_copy.wait()
    for copy in ops_copies:
        copy.wait()

    def loads_at(g):
        return jnp.concatenate([proj[slot_ref[0, g * face + k]] for k in range(face)], axis=0)

    def first_outer(step, carry):
        f = (step + 2) % 4
        put(ybuf, f, loads_at(f) - product(f))
        start_halo(f, 0)
        return carry

    def first_inner(g, carry):
        put(ybuf, g, loads_at(g) - product(g))
        return carry

    lax.fori_loop(0, 4, first_outer, 0)
    lax.fori_loop(4, 8, first_inner, 0)
    columns = call.shape[-1]
    chunk = nmode * LANES // 2
    if columns % chunk:
        chunk = columns
    padded = chunk // nmode * PAD
    place_rows = lax.broadcasted_iota(jnp.int32, (chunk, padded), 0)
    place_cols = lax.broadcasted_iota(jnp.int32, (chunk, padded), 1)
    group, mode = place_cols >> 3, place_cols & (PAD - 1)
    place = jnp.where((place_rows == group * nmode + mode) & (mode < nmode), 1.0, 0.0).astype(F32)
    for k in range(columns // chunk):
        high, low = split(jnp.dot(
            cfull[:, k * chunk:(k + 1) * chunk], place, precision=highest, preferred_element_type=F32))
        cpad[0:5 * unit, k * padded:(k + 1) * padded] = high
        cpad[5 * unit:10 * unit, k * padded:(k + 1) * padded] = low
    _, coeff = gather(0, fold(image_terms(0)))
    wait_halo_sent(0)
    side = spread_side(coeff)
    part = jnp.zeros((8, width), F32)
    for g in range(8):
        value = assembled(g, 0)
        put(res, g, value)
        value = value - correct(g, side)
        put(dire, g, value)
        part = part + weight(g) * rows8(value * value)
    gamma = None

    for iteration in range(ITERS):
        par = (iteration + 1) % 2
        last = iteration + 1 == ITERS
        load_side(dire)

        def outer(step, carry):
            f = (step + 2) % 4
            value = product(f)
            put(ybuf, f, value)
            start_halo(f, par)
            return carry + rows8(value * at(dire, f))

        def inner(g, carry):
            value = product(g)
            put(ybuf, g, value)
            return carry + rows8(value * at(dire, g))

        curv = lax.fori_loop(0, 4, outer, jnp.zeros((8, width), F32))
        curv = lax.fori_loop(4, 8, inner, curv)
        curv = jnp.sum(curv, axis=0, keepdims=True)
        message = jnp.where(row_ids == PAD - 2, curv, fold(image_terms(par)))
        if gamma is None:
            message = jnp.where(row_ids == PAD - 1, jnp.sum(part, axis=0, keepdims=True), message)
        sums, coeff_image = gather(par, message)
        wait_halo_sent(par)
        if gamma is None:
            gamma = sums[PAD - 1:PAD]
        length = gamma / sums[PAD - 2:PAD - 1]
        coeff = coeff - length * coeff_image
        side = spread_side(coeff)
        part = jnp.zeros((8, width), F32)
        for g in range(8):
            value = at(res, g) - length * assembled(g, par)
            if not last:
                put(res, g, value)
            value = value - correct(g, side)
            put(proj, g, value)
            if not last:
                part = part + weight(g) * rows8(value * value)
        if last:
            for b in range(nblk):
                s = inv_ref[b]
                res[b] = mult[s] + length * dire[s]
            mult_copy = pltpu.make_async_copy(res, out_ref.at[0], loads_sem)
            mult_copy.start()
            for b in range(nblk):
                ybuf[b] = proj[inv_ref[b]]
            proj_copy = pltpu.make_async_copy(ybuf, out_ref.at[1], ops_sem.at[0])
            proj_copy.start()
            mult_copy.wait()
            proj_copy.wait()
        else:
            def step_multipliers():
                for g in range(8):
                    put(mult, g, at(mult, g) + length * at(dire, g))

            following = total(part, step_multipliers)
            ratio = following / gamma
            gamma = following
            for g in range(8):
                put(dire, g, at(proj, g) + ratio * at(dire, g))


def solution(mesh):
    nc, ns = mesh.shape["cluster"], mesh.shape["sub"]
    devices = nc * ns

    def on_device(dual_operators, local_loads, modes, coarse_matrix, coarse_loads, slot_block):
        parts, order, loads = local_loads.shape
        nmode = modes.shape[1]
        slots = slot_block[0]
        nblk = slots.shape[0]
        face = nblk // 8
        blk = order * parts // nblk
        unit = parts * PAD
        positions = jnp.arange(nblk, dtype=jnp.int32)
        inverse = jnp.sum(
            positions[:, None] * (slots[:, None] == positions[None, :]).astype(jnp.int32), axis=0)
        vmem = pl.BlockSpec(memory_space=pltpu.VMEM)
        smem = pl.BlockSpec(memory_space=pltpu.SMEM)
        anym = pl.BlockSpec(memory_space=pl.ANY)
        vec = pltpu.VMEM((nblk, blk, loads), F32)
        dma = pltpu.SemaphoreType.DMA
        out = jax.ShapeDtypeStruct((2, nblk, blk, loads), F32)
        both = pl.pallas_call(
            functools.partial(kernel, nc, ns, parts, face),
            out_shape=out,
            in_specs=[smem, smem, anym, anym, vmem, vmem, vmem],
            out_specs=anym,
            scratch_shapes=[
                pltpu.VMEM((nblk, blk, order), BF16),
                vec, vec, vec, vec, vec,
                pltpu.VMEM((8, face * blk, 2 * LANES), BF16),
                pltpu.VMEM((order, parts * loads), BF16),
                pltpu.VMEM((2, 4, face, blk, loads), F32),
                pltpu.VMEM((nblk, PAD, blk), F32),
                pltpu.VMEM((nblk, unit, blk), F32),
                pltpu.VMEM((4, face, unit, blk), F32),
                pltpu.VMEM((8, 2 * unit, face * blk), BF16),
                pltpu.VMEM((5, unit, coarse_matrix.shape[1]), F32),
                pltpu.VMEM((10 * unit, devices * unit), BF16),
                pltpu.VMEM((2, nc, ns, unit, loads), F32),
                pltpu.VMEM((nc, 8, loads), F32),
                pltpu.VMEM((ns, 8, loads), F32),
                dma((8,)), dma(()),
                dma((4,)), dma((2, 4)), dma((4,)), dma((4,)), dma((4,)), dma((4,)),
                dma((nc,)), dma((2, nc)), dma((ns,)), dma((2, ns)), dma((nc,)), dma((ns,)),
            ],
            compiler_params=pltpu.CompilerParams(
                collective_id=0, has_side_effects=True, vmem_limit_bytes=56 * 1024 * 1024),
            cost_estimate=pl.CostEstimate(
                flops=8 * parts * order * order * loads, bytes_accessed=24 * 1024 * 1024, transcendentals=0),
        )(slot_block, inverse, dual_operators.reshape(nblk, blk, order),
          local_loads.reshape(nblk, blk, loads), modes.transpose(1, 0, 2), coarse_matrix, coarse_loads)
        return both[0].reshape(local_loads.shape), both[1].reshape(local_loads.shape)

    return jax.shard_map(
        on_device,
        mesh=mesh,
        in_specs=(
            P(("cluster", "sub"), None, None),
            P(("cluster", "sub"), None, None),
            P(("cluster", "sub"), None, None),
            P(("cluster", "sub"), None),
            P(),
            P(("cluster", "sub"), None),
        ),
        out_specs=(P(("cluster", "sub"), None, None), P(("cluster", "sub"), None, None)),
        check_vma=False,
    )
```
